512 devices in a mesh: row: 32 (over z, y_hi), col: 16 (over y_lo, x, core).
Axes of the slice: x: 4, y: 8 (y_hi: 4, y_lo: 2; y = y_hi * 2 + y_lo), z: 8, core: 2. Of those that a mesh axis runs over, the one named last changes fastest.
Arguments:
- orbitals: bfloat16 [20480, 384], P(('row', 'col')), may hold values from -6 to 6
- coulomb: float32 [20480, 20480], P('row', 'col'), may hold values from -0.001953125 to 0.001953125
- interp: bfloat16 [16384, 20480], P('row', 'col'), may hold values from -0.0390625 to 0.0390625
Outputs:
- exchanged: bfloat16 [16384, 384], P(('row', 'col'))
The draws below stay inside these ranges and needn't reach their ends.
All inputs are finite; a program needn't handle non-finite values.
Results may differ from the reference program's by a relative error of at most 0.018.
Values may be sent and summed in bfloat16 or wider, within the bound.
A program may use at most 64 MiB of HBM per device.

```python
import math
import jax
import jax.numpy as jnp
from jax import lax

NMU = 20480
NORB = 384
GRID = 16384


def block_scale(rng, dims, cuts, low, top_value):
    factor_of, own = 1.0, jax.random.fold_in(rng, 6)
    for position, parts in cuts:
        steps = jnp.exp(jax.random.uniform(jax.random.fold_in(own, position), (parts,), jnp.float32, low / len(cuts), top_value / len(cuts)))
        factor_of = factor_of * jnp.repeat(steps, dims[position] // parts).reshape([-1 if axis == position else 1 for axis in range(len(dims))])
    return factor_of


def noise(own_key, shape, deviation, bound, split=(), kind=jnp.bfloat16):
    drawn = jax.random.normal(own_key, shape, jnp.float32) * deviation
    if len(split) > 0:
        drawn = block_scale(own_key, shape, split, -0.22, 0.18) * drawn
    return jnp.clip(drawn, min=-bound, max=bound).astype(kind)


def setup_inputs(seed: int = 0) -> dict:
    streams_of = jax.random.split(jax.random.key(seed), 4)
    return {
        "orbitals": noise(streams_of[0], (NMU, NORB), 1.0, 6.0, ((0, 512),)),
        "coulomb": noise(streams_of[1], (NMU, NMU), (1.0 / (NORB * NMU) ** 0.5), 0.001953125, ((0, 32), (1, 16)), jnp.float32),
        "interp": noise(streams_of[2], (GRID, NMU), NMU ** -0.5, 0.0390625, ((0, 32), (1, 16))),
    }


def reference(orbitals, coulomb, interp):
    block = math.gcd(NMU, 512)

    def step(total, index):
        start = (index * block).astype(jnp.int32)
        rows = lax.dynamic_slice_in_dim(orbitals, start, block, 0)
        kernel = lax.dynamic_slice_in_dim(coulomb, start, block, 0)
        density = jnp.dot(rows, orbitals.T, preferred_element_type=jnp.float32)
        weighted = (kernel * density).astype(jnp.bfloat16)
        return total + jnp.dot(weighted.T, rows, preferred_element_type=jnp.float32), None

    total, unused = lax.scan(step, jnp.zeros((NMU, NORB), jnp.float32), jnp.arange(NMU // block, dtype=jnp.int32))
    contracted = total.astype(jnp.bfloat16)
    return jnp.dot(interp, contracted, preferred_element_type=jnp.float32).astype(jnp.bfloat16)
```

```python
import jax
import jax.numpy as jnp
from jax import lax
from jax.experimental import pallas as pl
from jax.experimental.pallas import tpu as pltpu
from jax.sharding import PartitionSpec as P

MESH = pl.DeviceIdType.MESH
Z, Y, L, X, C = 8, 4, 2, 4, 2
F32, BF16 = jnp.float32, jnp.bfloat16


def device(z, y, l, x, core):
    return (z * Y + y, (l * X + x) * C + core)


def rows(slots):
    n, h, k = slots.shape
    return slots.astype(F32).reshape(n * h, k)


def kernel(
    orb, coul_hbm, interp_hbm, out,
    coul, coul_t, interp, near_s, near, far, acc_in, acc_out, part,
    y_out, y_in, con, con_m, terms, pair_out, pair_in, fin_out, fin_in,
    local_sem, near_ss, near_rs, sib_ss, sib_rs, perm_ss, perm_rs,
    far_ss, far_rs, acc_ss, acc_rs, ys_ss, ys_rs, yg_ss, yg_rs,
    con_ss, con_rs, pair_sem, fin_ss, fin_rs,
):
    row, col = lax.axis_index("row"), lax.axis_index("col")
    z, y = row // Y, row % Y
    l, x, core = col // (X * C), (col // C) % X, col % C
    up, down = device((z + 1) % Z, y, l, x, core), device((z + Z - 1) % Z, y, l, x, core)
    sibling = device(z, y, l, x, 1 - core)
    chips = [None] + [((l + k // X) % L, (x + k % X) % X) for k in range(1, L * X)]
    came = [None] + [((l + k // X) % L, (x + X - k % X) % X) for k in range(1, L * X)]
    ahead = [None] + [(y + k) % Y for k in range(1, Y)]
    behind = [None] + [(y + Y - k) % Y for k in range(1, Y)]
    sends = []

    def send(src, dst, ss, rs, to):
        copy = pltpu.make_async_remote_copy(
            src_ref=src, dst_ref=dst, send_sem=ss, recv_sem=rs, device_id=to, device_id_type=MESH
        )
        copy.start()
        sends.append(copy)
        return copy

    load_coul = pltpu.make_async_copy(coul_hbm, coul, local_sem.at[0])
    load_interp = pltpu.make_async_copy(interp_hbm, interp, local_sem.at[1])
    load_coul.start()
    load_interp.start()

    piece = (row % 2) * (L * X * C) + col
    target_col, target_z = row // 2, piece // Y
    targets = [(target_z * Y + j, target_col) for j in range(Y)]
    target_self = [(t[0] == row) & (t[1] == col) for t in targets]
    sources = []
    for j in range(Y):
        p = z * Y + j
        sources.append((2 * col + p // (L * X * C), p % (L * X * C)))
    source_self = [(s[0] == row) & (s[1] == col) for s in sources]

    barrier = pltpu.get_barrier_semaphore()
    greet = [up, down, sibling]
    greet += [device(z, y, chips[k][0], chips[k][1], core) for k in range(1, L * X)]
    greet += [device(z, ahead[k], l, x, core) for k in range(1, Y)]
    for d in greet:
        pl.semaphore_signal(barrier, inc=1, device_id=d, device_id_type=MESH)
    for j in range(Y):
        @pl.when(jnp.logical_not(source_self[j]))
        def _(j=j):
            pl.semaphore_signal(barrier, inc=1, device_id=sources[j], device_id_type=MESH)
    own_target = (target_col == col) & (target_z == z)
    pl.semaphore_wait(barrier, jnp.where(own_target, len(greet) + Y - 1, len(greet) + Y))

    kind = piece % Y

    def perm(j):
        return pltpu.make_async_remote_copy(
            src_ref=orb, dst_ref=far.at[piece], send_sem=perm_ss.at[j], recv_sem=perm_rs.at[kind],
            device_id=targets[j], device_id_type=MESH,
        )

    for j in range(Y):
        @pl.when(jnp.logical_not(target_self[j]))
        def _(j=j):
            perm(j).start()

        @pl.when(target_self[j])
        def _():
            far[piece] = orb[...]

    near_s[col] = orb[...]
    sib = [send(orb, near_s.at[col], sib_ss.at[0], sib_rs.at[0], sibling)]
    near_c = [None]
    for k in range(1, L * X):
        near_c.append(send(orb, near_s.at[col], near_ss.at[k], near_rs.at[k], device(z, y, *chips[k], core)))

    load_coul.wait()
    for k in range(coul.shape[1] // 128):
        coul_t[pl.ds(128 * k, 128), :] = coul[:, pl.ds(128 * k, 128)].T

    for k in range(1, L * X):
        near_c[k].wait_recv()
        slot = (came[k][0] * X + came[k][1]) * C + core
        sib.append(send(near_s.at[slot], near_s.at[slot], sib_ss.at[k], sib_rs.at[k], sibling))

    for j in range(Y):
        @pl.when(jnp.logical_not(source_self[j]))
        def _(j=j):
            pltpu.make_async_remote_copy(
                src_ref=orb, dst_ref=far.at[z * Y + j], send_sem=perm_ss.at[j], recv_sem=perm_rs.at[j],
                device_id=sources[j], device_id_type=MESH,
            ).wait_recv()

    def far_send(way, step, first, count):
        at = pl.ds(first, count)
        return send(far.at[at], far.at[at], far_ss.at[way, step], far_rs.at[way, step], (up, down)[way])

    far_c = [[far_send(0, 0, z * Y, Y)], [far_send(1, 0, z * Y, Y)]]
    for c in sib:
        c.wait_recv()
    near[...] = rows(near_s[...]).astype(BF16)

    def partial(block):
        points = rows(far[pl.ds(block * Y, Y)]).astype(BF16)
        density = lax.dot_general(points, near[...], (((1,), (1,)), ((), ())), preferred_element_type=F32)
        n = points.shape[0]
        weighted = (coul_t[pl.ds(pl.multiple_of(block * n, n), n), :] * density).astype(BF16)
        return jnp.dot(weighted, near[...], preferred_element_type=F32).reshape(Y, n // Y, -1)

    half = Y // 2
    own = partial(z)
    acc_out[0, 0, :half] = own[:half].astype(BF16)
    acc_out[1, 0, half:] = own[half:].astype(BF16)
    acc_c = [[], []]
    for way in range(2):
        at = pl.ds(half * way, half)
        acc_c[way].append(send(
            acc_out.at[way, 0, at], acc_in.at[way, 0, at],
            acc_ss.at[way, 0], acc_rs.at[way, 0], (up, down)[way]))
    for step in range(1, 4):
        blocks = ((z + Z - step) % Z, (z + step) % Z)
        for way in range(2):
            far_c[way][step - 1].wait_recv()
            if step < 3:
                far_c[way].append(far_send(way, step, blocks[way] * Y, Y))
            else:
                far_c[way].append(far_send(way, step, blocks[way] * Y + half * way, half))
        for way in range(2):
            share = partial(blocks[way])
            acc_c[way][step - 1].wait_recv()
            if step == 1:
                lo, hi = half * way, half * (way + 1)
                rest = slice(half, Y) if way == 0 else slice(0, half)
                acc_out[way, step, lo:hi] = (share[lo:hi] + acc_in[way, 0, lo:hi].astype(F32)).astype(BF16)
                acc_out[way, step, rest] = share[rest].astype(BF16)
            else:
                acc_out[way, step] = (share + acc_in[way, step - 1].astype(F32)).astype(BF16)
            acc_c[way].append(send(
                acc_out.at[way, step], acc_in.at[way, step],
                acc_ss.at[way, step], acc_rs.at[way, step], (up, down)[way]))
    far_c[0][3].wait_recv()
    far_c[1][3].wait_recv()
    block = (z + Z // 2) % Z
    share = partial(block)
    acc_c[0][3].wait_recv()
    acc_c[1][3].wait_recv()
    share = share + acc_in[0, 3].astype(F32) + acc_in[1, 3].astype(F32)
    part[...] = share
    y_out[...] = share.astype(BF16)

    ys = [None]
    for k in range(1, Y):
        ys.append(send(y_out.at[ahead[k]], y_in.at[k], ys_ss.at[k], ys_rs.at[k], device(z, ahead[k], l, x, core)))
    total = part[y]
    for k in range(1, Y):
        ys[k].wait_recv()
        total = total + y_in[k].astype(F32)
    mine = block * Y + y
    con[mine] = total.astype(BF16)
    yg = [None]
    for k in range(1, Y):
        yg.append(send(con.at[mine], con.at[mine], yg_ss.at[k], yg_rs.at[k], device(z, ahead[k], l, x, core)))
    for k in range(1, Y):
        yg[k].wait_recv()

    def con_send(way, step, first, count):
        at = pl.ds(first, count)
        return send(con.at[at], con.at[at], con_ss.at[way, step], con_rs.at[way, step], (up, down)[way])

    con_c = [[con_send(0, 0, block * Y, Y)], [con_send(1, 0, block * Y, Y)]]
    for step in range(1, 4):
        blocks = ((block + Z - step) % Z, (block + step) % Z)
        for way in range(2):
            con_c[way][step - 1].wait_recv()
            if step < 3:
                con_c[way].append(con_send(way, step, blocks[way] * Y, Y))
            else:
                con_c[way].append(con_send(way, step, blocks[way] * Y + half * way, half))
    load_interp.wait()
    con_c[0][3].wait_recv()
    con_c[1][3].wait_recv()
    con_m[...] = rows(con[...]).astype(BF16)
    terms[...] = jnp.dot(interp[...], con_m[...], preferred_element_type=F32).reshape(terms.shape)

    pair_out[...] = terms[:, 1 - core].astype(BF16)
    pair = send(pair_out, pair_in, pair_sem.at[0], pair_sem.at[1], sibling)
    pair.wait_recv()
    both = terms[:, core] + pair_in[...].astype(F32)
    terms[:, core] = both
    fin_out[...] = both.astype(BF16)
    fin = [None]
    for k in range(1, L * X):
        fin.append(send(
            fin_out.at[chips[k][0] * X + chips[k][1]], fin_in.at[k],
            fin_ss.at[k], fin_rs.at[k], device(z, y, *chips[k], core)))
    total = terms[l * X + x, core]
    for k in range(1, L * X):
        fin[k].wait_recv()
        total = total + fin_in[k].astype(F32)
    out[...] = total.astype(BF16)

    for c in sends:
        c.wait_send()
    for j in range(Y):
        @pl.when(jnp.logical_not(target_self[j]))
        def _(j=j):
            perm(j).wait_send()


def local(orbitals, coulomb, interp):
    h, k = orbitals.shape
    m, n = coulomb.shape
    g = interp.shape[0]
    out = g // (L * X * C)
    dma = pltpu.SemaphoreType.DMA
    return pl.pallas_call(
        kernel,
        out_shape=jax.ShapeDtypeStruct((out, k), BF16),
        in_specs=[
            pl.BlockSpec(memory_space=pltpu.VMEM),
            pl.BlockSpec(memory_space=pl.ANY),
            pl.BlockSpec(memory_space=pl.ANY),
        ],
        out_specs=pl.BlockSpec(memory_space=pltpu.VMEM),
        scratch_shapes=[
            pltpu.VMEM((m, n), F32),
            pltpu.VMEM((n, m), F32),
            pltpu.VMEM((g, n), BF16),
            pltpu.VMEM((L * X * C, h, k), BF16),
            pltpu.VMEM((m, k), BF16),
            pltpu.VMEM((Z * Y, h, k), BF16),
            pltpu.VMEM((2, 4, Y, h, k), BF16),
            pltpu.VMEM((2, 4, Y, h, k), BF16),
            pltpu.VMEM((Y, h, k), F32),
            pltpu.VMEM((Y, h, k), BF16),
            pltpu.VMEM((Y, h, k), BF16),
            pltpu.VMEM((Z * Y, h, k), BF16),
            pltpu.VMEM((n, k), BF16),
            pltpu.VMEM((L * X, C, out, k), F32),
            pltpu.VMEM((L * X, out, k), BF16),
            pltpu.VMEM((L * X, out, k), BF16),
            pltpu.VMEM((L * X, out, k), BF16),
            pltpu.VMEM((L * X, out, k), BF16),
            dma((2,)), dma((8,)), dma((8,)), dma((8,)), dma((8,)), dma((4,)), dma((4,)),
            dma((2, 4)), dma((2, 4)), dma((2, 4)), dma((2, 4)), dma((4,)), dma((4,)), dma((4,)), dma((4,)),
            dma((2, 4)), dma((2, 4)), dma((2,)), dma((8,)), dma((8,)),
        ],
        compiler_params=pltpu.CompilerParams(
            collective_id=0, has_side_effects=True, vmem_limit_bytes=40 * 1024 * 1024
        ),
        cost_estimate=pl.CostEstimate(
            flops=4 * m * n * k + 2 * g * n * k, bytes_accessed=4 * m * n + 2 * g * n, transcendentals=0
        ),
    )(orbitals, coulomb, interp)


def solution(mesh):
    in_specs = (P(("row", "col"), None), P("row", "col"), P("row", "col"))
    out_specs = P(("row", "col"), None)
    return jax.shard_map(local, mesh=mesh, in_specs=in_specs, out_specs=out_specs, check_vma=False)
```

```python
import jax
import jax.numpy as jnp
from jax import lax
from jax.experimental import pallas as pl
from jax.experimental.pallas import tpu as pltpu
from jax.sharding import PartitionSpec as P

MESH = pl.DeviceIdType.MESH
Z, Y, L, X, C = 8, 4, 2, 4, 2
F32, BF16 = jnp.float32, jnp.bfloat16
H = 2


def device(z, y, l, x, core):
    return (z * Y + y, (l * X + x) * C + core)


def side_of(turn):
    return (2 + X - turn // C) % X


def core_of(turn):
    return (turn + turn // X) % C


def turn_of(side, core):
    half = (2 + X - side) % X
    return half * C + (core + half // 2) % C


def rows(slots):
    n, h, k = slots.shape
    return slots.astype(F32).reshape(n * h, k)


def kernel(
    orb, coul_hbm, interp_hbm, out,
    coul, coul_t, interp, near_s, near, far, acc_in, acc_out, part,
    y_out, y_in, con, con_f, con_m, relay, terms, pair_out, pair_in, fin_out, fin_in,
    local_sem, relay_sem, near_ss, near_rs, sib_ss, sib_rs, perm_ss, perm_rs,
    far_ss, far_rs, acc_ss, acc_rs, ys_ss, ys_rs, yg_ss, yg_rs,
    con_ss, con_rs, pair_sem, fin_ss, fin_rs,
):
    row, col = lax.axis_index("row"), lax.axis_index("col")
    z, y = row // Y, row % Y
    l, x, core = col // (X * C), (col // C) % X, col % C
    up, down = device((z + 1) % Z, y, l, x, core), device((z + Z - 1) % Z, y, l, x, core)
    up2, down2 = device((z + 2) % Z, y, l, x, core), device((z + Z - 2) % Z, y, l, x, core)
    sibling = device(z, y, l, x, 1 - core)
    chips = [None] + [((l + k // X) % L, (x + k % X) % X) for k in range(1, L * X)]
    came = [None] + [((l + k // X) % L, (x + X - k % X) % X) for k in range(1, L * X)]
    ahead = [None] + [(y + k) % Y for k in range(1, Y)]
    behind = [None] + [(y + Y - k) % Y for k in range(1, Y)]
    sends = []

    def send(src, dst, ss, rs, to):
        copy = pltpu.make_async_remote_copy(
            src_ref=src, dst_ref=dst, send_sem=ss, recv_sem=rs, device_id=to, device_id_type=MESH
        )
        copy.start()
        sends.append(copy)
        return copy

    load_coul = pltpu.make_async_copy(coul_hbm, coul, local_sem.at[0])
    load_interp = pltpu.make_async_copy(interp_hbm, interp, local_sem.at[1])
    load_coul.start()
    load_interp.start()

    home = (z + Z - col // C) % Z
    turn = turn_of((x + X - z % X) % X, core)
    first_to = device((z + turn) % Z, y, l, z % X, core)
    relayed = (z + Z - x) % Z
    other = jnp.where(core_of(relayed) == core, 0, 1)
    relayed = (relayed + other * X) % Z
    first_from = device(x + other * X, y, l, (x + side_of(relayed)) % X, core)
    piece = relayed * Y + (y % 2) * L + l
    targets = [device(z, j, other, x, y // 2) for j in range(Y)]
    own_target = (other == l) & (y // 2 == core)
    target_self = [own_target & (y == j) for j in range(Y)]
    sources = [device(z, core * 2 + j // L, j % L, x, core_of(home)) for j in range(Y)]
    source_self = [(s[0] == row) & (s[1] == col) for s in sources]

    barrier = pltpu.get_barrier_semaphore()
    greet = [first_from] + [device(z, y, *chips[k], core) for k in range(1, L * X)] + [sibling, up, down, up2, down2]
    greet += [device(z, ahead[k], l, x, core) for k in range(1, Y)]
    for j in range(Y):
        @pl.when(jnp.logical_not(source_self[j]))
        def _(j=j):
            pl.semaphore_signal(barrier, inc=1, device_id=sources[j], device_id_type=MESH)
    for d in greet:
        pl.semaphore_signal(barrier, inc=1, device_id=d, device_id_type=MESH)
    pl.semaphore_wait(barrier, jnp.where(own_target, len(greet) + Y - 1, len(greet) + Y))

    kind = piece % Y
    relay_c = send(orb, relay, relay_sem.at[0], relay_sem.at[1], first_to)

    def perm(j):
        return pltpu.make_async_remote_copy(
            src_ref=relay, dst_ref=far.at[piece], send_sem=perm_ss.at[j], recv_sem=perm_rs.at[kind],
            device_id=targets[j], device_id_type=MESH,
        )

    def finish():
        for c in sends:
            c.wait_send()
        for j in range(Y):
            @pl.when(jnp.logical_not(target_self[j]))
            def _(j=j):
                perm(j).wait_send()

    near_s[col] = orb[...]
    sib = [send(orb, near_s.at[col], sib_ss.at[0], sib_rs.at[0], sibling)]
    near_c = [None]
    for k in range(1, L * X):
        near_c.append(send(orb, near_s.at[col], near_ss.at[k], near_rs.at[k], device(z, y, *chips[k], core)))

    relay_c.wait_recv()
    for j in range(Y):
        @pl.when(jnp.logical_not(target_self[j]))
        def _(j=j):
            perm(j).start()

        @pl.when(target_self[j])
        def _():
            far[piece] = relay[...]

    load_coul.wait()
    for k in range(coul.shape[1] // 128):
        coul_t[pl.ds(128 * k, 128), :] = coul[:, pl.ds(128 * k, 128)].T

    parts = range(H)
    span = Y // H
    held = (range(H // 2), range(H // 2, H))

    def far_send(way, step, block, h):
        at = pl.ds(block * Y + h * span, span)
        return send(far.at[at], far.at[at], far_ss.at[way, step, h], far_rs.at[way, step, h], (up, down)[way])

    def acc_send(way, step, h):
        at = pl.ds(h * span, span)
        return send(
            acc_out.at[way, step, at], acc_in.at[way, step, at],
            acc_ss.at[way, step, h], acc_rs.at[way, step, h], (up, down)[way])

    def place(block, j):
        n = orb.shape[0]
        p = (j // L) * (L * X * C) + (j % L) * (X * C) + ((x + side_of(block)) % X) * C + core_of(block)
        return pl.ds(pl.multiple_of(p * n, n), n)

    def partial(block):
        points = rows(far[pl.ds(block * Y, Y)]).astype(BF16)
        density = lax.dot_general(points, near[...], (((1,), (1,)), ((), ())), preferred_element_type=F32)
        n = points.shape[0] // Y
        factor = jnp.concatenate([coul_t[place(block, j), :] for j in range(Y)], 0)
        weighted = (factor * density).astype(BF16)
        return jnp.dot(weighted, near[...], preferred_element_type=F32).reshape(Y, n, -1)

    far_c, acc_c = {}, {}
    for j in range(Y):
        @pl.when(jnp.logical_not(source_self[j]))
        def _(j=j):
            pltpu.make_async_remote_copy(
                src_ref=orb, dst_ref=far.at[home * Y + j], send_sem=perm_ss.at[j], recv_sem=perm_rs.at[j],
                device_id=sources[j], device_id_type=MESH,
            ).wait_recv()

        if (j + 1) % span == 0:
            for way in range(2):
                far_c[way, 0, j // span] = far_send(way, 0, home, j // span)
    for k in range(1, L * X):
        near_c[k].wait_recv()
        slot = (came[k][0] * X + came[k][1]) * C + core
        sib.append(send(near_s.at[slot], near_s.at[slot], sib_ss.at[k], sib_rs.at[k], sibling))

    for c in sib:
        c.wait_recv()
    near[...] = rows(near_s[...]).astype(BF16)

    own = partial(home)
    for way in range(2):
        for h in held[way]:
            at = slice(h * span, (h + 1) * span)
            acc_out[way, 0, at] = own[at].astype(BF16)
            acc_c[way, 0, h] = acc_send(way, 0, h)
    for step in range(1, 4):
        blocks = ((home + Z - step) % Z, (home + step) % Z)
        for h in parts:
            for way in range(2):
                far_c[way, step - 1, h].wait_recv()
                if step < 3 or h in held[way]:
                    far_c[way, step, h] = far_send(way, step, blocks[way], h)
        shares = [partial(blocks[way]) for way in range(2)]
        for h in parts:
            at = slice(h * span, (h + 1) * span)
            for way in range(2):
                share = shares[way][at]
                if (way, step - 1, h) in acc_c:
                    acc_c[way, step - 1, h].wait_recv()
                    share = share + acc_in[way, step - 1, at].astype(F32)
                acc_out[way, step, at] = share.astype(BF16)
                acc_c[way, step, h] = acc_send(way, step, h)
    for way in range(2):
        for h in held[way]:
            far_c[way, 3, h].wait_recv()
    block = (home + Z // 2) % Z
    share = partial(block)
    for h in parts:
        at = slice(h * span, (h + 1) * span)
        for way in range(2):
            acc_c[way, 3, h].wait_recv()
        total = share[at] + acc_in[0, 3, at].astype(F32) + acc_in[1, 3, at].astype(F32)
        part[at] = total
        y_out[at] = total.astype(BF16)

    ys = [None]
    for k in range(1, Y):
        ys.append(send(y_out.at[ahead[k]], y_in.at[k], ys_ss.at[k], ys_rs.at[k], device(z, ahead[k], l, x, core)))
    total = part[y]
    for k in range(1, Y):
        ys[k].wait_recv()
        total = total + y_in[k].astype(F32)
    mine = block * Y + y
    con[mine] = total.astype(BF16)
    def con_send(way, step, back, k):
        slot = ((block + (Z - back, back)[way]) % Z) * Y + spot[k]
        to = ((up, up2, up, up2), (down, down2, down, down2))[way][step]
        return send(con.at[slot], con.at[slot], con_ss.at[way, step, k], con_rs.at[way, step, k], to)

    spot = [y] + behind[1:]
    yg, con_c = {}, {}
    for k in (2, 1, 3):
        yg[k] = send(con.at[mine], con.at[mine], yg_ss.at[k], yg_rs.at[k], device(z, ahead[k], l, x, core))

    def begin(k):
        if k > 0:
            yg[k].wait_recv()
        for step in (1, 0):
            for way in range(2):
                con_c[way, step, k] = con_send(way, step, 0, k)

    def forward(k):
        for way in range(2):
            con_c[way, 1, k].wait_recv()
            if (k < 2) == (way == 0):
                con_c[way, 3, k] = con_send(way, 3, 2, k)
            con_c[way, 2, k] = con_send(way, 2, 2, k)

    def settle(b):
        for j in range(Y):
            con_f[place(b, j), :] = con[b * Y + j].astype(F32)

    begin(0)
    begin(1)
    begin(3)
    forward(0)
    begin(2)
    settle(block)
    for k in (1, 3, 2):
        forward(k)
    for way in range(2):
        for k in range(Y):
            con_c[way, 0, k].wait_recv()
        settle((block + (Z - 1, 1)[way]) % Z)
        settle((block + (Z - 2, 2)[way]) % Z)
    for way in range(2):
        for k in range(Y):
            con_c[way, 2, k].wait_recv()
        settle((block + (Z - 3, 3)[way]) % Z)
    load_interp.wait()
    for k in range(Y):
        con_c[0 if k < 2 else 1, 3, k].wait_recv()
    settle((block + 4) % Z)
    con_m[...] = con_f[...].astype(BF16)

    def term(half):
        tile = interp[:, half]
        return jnp.dot(tile.reshape(-1, tile.shape[-1]), con_m[...], preferred_element_type=F32).reshape(terms.shape)

    pair_out[...] = term(1 - core).astype(BF16)
    pair = send(pair_out, pair_in, pair_sem.at[0], pair_sem.at[1], sibling)
    both = term(core)
    pair.wait_recv()
    both = both + pair_in[...].astype(F32)
    terms[...] = both
    fin_out[...] = both.astype(BF16)
    fin = [None]
    for k in range(1, L * X):
        fin.append(send(
            fin_out.at[chips[k][0] * X + chips[k][1]], fin_in.at[k],
            fin_ss.at[k], fin_rs.at[k], device(z, y, *chips[k], core)))
    total = terms[l * X + x]
    for k in range(1, L * X):
        fin[k].wait_recv()
        total = total + fin_in[k].astype(F32)
    out[...] = total.astype(BF16)

    finish()


def local(orbitals, coulomb, interp):
    h, k = orbitals.shape
    m, n = coulomb.shape
    g = interp.shape[0]
    out = g // (L * X * C)
    dma = pltpu.SemaphoreType.DMA
    return pl.pallas_call(
        kernel,
        out_shape=jax.ShapeDtypeStruct((out, k), BF16),
        in_specs=[
            pl.BlockSpec(memory_space=pltpu.VMEM),
            pl.BlockSpec(memory_space=pltpu.HBM),
            pl.BlockSpec(memory_space=pltpu.HBM),
        ],
        out_specs=pl.BlockSpec(memory_space=pltpu.VMEM),
        scratch_shapes=[
            pltpu.VMEM((m, n), F32),
            pltpu.VMEM((n, m), F32),
            pltpu.VMEM((L * X, C, out, n), BF16),
            pltpu.VMEM((L * X * C, h, k), BF16),
            pltpu.VMEM((m, k), BF16),
            pltpu.VMEM((Z * Y, h, k), BF16),
            pltpu.VMEM((2, 4, Y, h, k), BF16),
            pltpu.VMEM((2, 4, Y, h, k), BF16),
            pltpu.VMEM((Y, h, k), F32),
            pltpu.VMEM((Y, h, k), BF16),
            pltpu.VMEM((Y, h, k), BF16),
            pltpu.VMEM((Z * Y, h, k), BF16),
            pltpu.VMEM((n, k), F32),
            pltpu.VMEM((n, k), BF16),
            pltpu.VMEM((h, k), BF16),
            pltpu.VMEM((L * X, out, k), F32),
            pltpu.VMEM((L * X, out, k), BF16),
            pltpu.VMEM((L * X, out, k), BF16),
            pltpu.VMEM((L * X, out, k), BF16),
            pltpu.VMEM((L * X, out, k), BF16),
            dma((2,)), dma((2,)), dma((8,)), dma((8,)), dma((8,)), dma((8,)), dma((4,)), dma((4,)),
            dma((2, 4, H)), dma((2, 4, H)), dma((2, 4, H)), dma((2, 4, H)), dma((4,)), dma((4,)), dma((4,)), dma((4,)),
            dma((2, 4, Y)), dma((2, 4, Y)), dma((2,)), dma((8,)), dma((8,)),
        ],
        compiler_params=pltpu.CompilerParams(
            collective_id=0, has_side_effects=True, vmem_limit_bytes=62 * 1024 * 1024
        ),
        cost_estimate=pl.CostEstimate(
            flops=4 * m * n * k + 2 * g * n * k, bytes_accessed=4 * m * n + 2 * g * n, transcendentals=0
        ),
    )(orbitals, coulomb, interp.reshape(L * X, C, out, n))


def solution(mesh):
    in_specs = (P(("row", "col"), None), P("row", "col"), P("row", "col"))
    out_specs = P(("row", "col"), None)
    return jax.shard_map(local, mesh=mesh, in_specs=in_specs, out_specs=out_specs, check_vma=False)
```

```python
import jax
import jax.numpy as jnp
from jax import lax
from jax.experimental import pallas as pl
from jax.experimental.pallas import tpu as pltpu
from jax.sharding import PartitionSpec as P

MESH = pl.DeviceIdType.MESH
Z, Y, L, X, C = 8, 4, 2, 4, 2
F32, BF16 = jnp.float32, jnp.bfloat16
H = 4


def device(z, y, l, x, core):
    return (z * Y + y, (l * X + x) * C + core)


def side_of(turn):
    return (2 + X - turn // C) % X


def core_of(turn):
    return (turn + turn // X) % C


def turn_of(side, core):
    half = (2 + X - side) % X
    return half * C + (core + half // 2) % C


def rows(slots):
    n, h, k = slots.shape
    return slots.astype(F32).reshape(n * h, k)


def kernel(
    orb, coul_hbm, interp_hbm, out,
    coul, coul_t, interp, near_s, near, far, acc_in, acc_out, part,
    y_out, y_in, con, con_f, con_m, relay, terms, pair_out, pair_in, fin_out, fin_in,
    local_sem, relay_sem, near_ss, near_rs, sib_ss, sib_rs, perm_ss, perm_rs,
    far_ss, far_rs, acc_ss, acc_rs, ys_ss, ys_rs,
    con_ss, con_rs, pair_ss, pair_rs, fin_ss, fin_rs,
):
    row, col = lax.axis_index("row"), lax.axis_index("col")
    z, y = row // Y, row % Y
    l, x, core = col // (X * C), (col // C) % X, col % C
    up, down = device((z + 1) % Z, y, l, x, core), device((z + Z - 1) % Z, y, l, x, core)
    plane = [device((z + d) % Z, y, l, x, core) for d in range(Z)]
    sibling = device(z, y, l, x, 1 - core)
    chips = [None] + [((l + k // X) % L, (x + k % X) % X) for k in range(1, L * X)]
    came = [None] + [((l + k // X) % L, (x + X - k % X) % X) for k in range(1, L * X)]
    ahead = [None] + [(y + k) % Y for k in range(1, Y)]
    behind = [None] + [(y + Y - k) % Y for k in range(1, Y)]
    sends = []

    def send(src, dst, ss, rs, to):
        copy = pltpu.make_async_remote_copy(
            src_ref=src, dst_ref=dst, send_sem=ss, recv_sem=rs, device_id=to, device_id_type=MESH
        )
        copy.start()
        sends.append(copy)
        return copy

    load_coul = pltpu.make_async_copy(coul_hbm, coul, local_sem.at[0])
    load_interp = pltpu.make_async_copy(interp_hbm, interp, local_sem.at[1])
    load_coul.start()
    load_interp.start()

    home = (z + Z - col // C) % Z
    turn = turn_of((x + X - z % X) % X, core)
    first_to = device((z + turn) % Z, y, l, z % X, core)
    relayed = (z + Z - x) % Z
    other = jnp.where(core_of(relayed) == core, 0, 1)
    relayed = (relayed + other * X) % Z
    first_from = device(x + other * X, y, l, (x + side_of(relayed)) % X, core)
    piece = relayed * Y + (y % 2) * L + l
    targets = [device(z, j, other, x, y // 2) for j in range(Y)]
    own_target = (other == l) & (y // 2 == core)
    target_self = [own_target & (y == j) for j in range(Y)]
    sources = [device(z, core * 2 + j // L, j % L, x, core_of(home)) for j in range(Y)]
    source_self = [(s[0] == row) & (s[1] == col) for s in sources]

    barrier = pltpu.get_barrier_semaphore()
    greet = [first_from] + [device(z, y, *chips[k], core) for k in range(1, L * X)] + [sibling] + plane[1:]
    greet += [device(z, ahead[k], l, x, core) for k in range(1, Y)]
    for j in range(Y):
        @pl.when(jnp.logical_not(source_self[j]))
        def _(j=j):
            pl.semaphore_signal(barrier, inc=1, device_id=sources[j], device_id_type=MESH)
    for d in greet:
        pl.semaphore_signal(barrier, inc=1, device_id=d, device_id_type=MESH)
    pl.semaphore_wait(barrier, jnp.where(own_target, len(greet) + Y - 1, len(greet) + Y))

    kind = piece % Y
    relay_c = send(orb, relay, relay_sem.at[0], relay_sem.at[1], first_to)

    def perm(j):
        return pltpu.make_async_remote_copy(
            src_ref=relay, dst_ref=far.at[piece], send_sem=perm_ss.at[j], recv_sem=perm_rs.at[kind],
            device_id=targets[j], device_id_type=MESH,
        )

    def finish():
        for c in sends:
            c.wait_send()
        for j in range(Y):
            @pl.when(y != j)
            def _(j=j):
                y_send(j).wait_send()
        for j in range(Y):
            @pl.when(jnp.logical_not(target_self[j]))
            def _(j=j):
                perm(j).wait_send()

    near_s[col] = orb[...]
    sib = [send(orb, near_s.at[col], sib_ss.at[0], sib_rs.at[0], sibling)]
    near_c = [None]
    for k in range(1, L * X):
        near_c.append(send(orb, near_s.at[col], near_ss.at[k], near_rs.at[k], device(z, y, *chips[k], core)))

    relay_c.wait_recv()
    for j in range(Y):
        @pl.when(jnp.logical_not(target_self[j]))
        def _(j=j):
            perm(j).start()

        @pl.when(target_self[j])
        def _():
            far[piece] = relay[...]

    load_coul.wait()
    for k in range(coul.shape[1] // 128):
        coul_t[pl.ds(128 * k, 128), :] = coul[:, pl.ds(128 * k, 128)].T

    parts = range(H)
    span = Y // H
    held = (range(H // 2), range(H // 2, H))

    def far_send(way, step, block, h):
        at = pl.ds(block * Y + h * span, span)
        return send(far.at[at], far.at[at], far_ss.at[way, step, h], far_rs.at[way, step, h], (up, down)[way])

    def acc_send(way, step, h):
        at = pl.ds(h * span, span)
        return send(
            acc_out.at[way, step, at], acc_in.at[way, step, at],
            acc_ss.at[way, step, h], acc_rs.at[way, step, h], (up, down)[way])

    def place(block, j):
        n = orb.shape[0]
        p = (j // L) * (L * X * C) + (j % L) * (X * C) + ((x + side_of(block)) % X) * C + core_of(block)
        return pl.ds(pl.multiple_of(p * n, n), n)

    def partial(block):
        points = rows(far[pl.ds(block * Y, Y)]).astype(BF16)
        density = lax.dot_general(points, near[...], (((1,), (1,)), ((), ())), preferred_element_type=F32)
        n = points.shape[0] // Y
        factor = jnp.concatenate([coul_t[place(block, j), :] for j in range(Y)], 0)
        weighted = (factor * density).astype(BF16)
        return jnp.dot(weighted, near[...], preferred_element_type=F32).reshape(Y, n, -1)

    far_c, acc_c = {}, {}
    for j in range(Y):
        @pl.when(jnp.logical_not(source_self[j]))
        def _(j=j):
            pltpu.make_async_remote_copy(
                src_ref=orb, dst_ref=far.at[home * Y + j], send_sem=perm_ss.at[j], recv_sem=perm_rs.at[j],
                device_id=sources[j], device_id_type=MESH,
            ).wait_recv()

        if (j + 1) % span == 0:
            for way in range(2):
                far_c[way, 0, j // span] = far_send(way, 0, home, j // span)
    for k in range(1, L * X):
        near_c[k].wait_recv()
        slot = (came[k][0] * X + came[k][1]) * C + core
        sib.append(send(near_s.at[slot], near_s.at[slot], sib_ss.at[k], sib_rs.at[k], sibling))

    for c in sib:
        c.wait_recv()
    near[...] = rows(near_s[...]).astype(BF16)

    own = partial(home)
    for way in range(2):
        for h in held[way]:
            at = slice(h * span, (h + 1) * span)
            acc_out[way, 0, at] = own[at].astype(BF16)
            acc_c[way, 0, h] = acc_send(way, 0, h)
    for step in range(1, 4):
        blocks = ((home + Z - step) % Z, (home + step) % Z)
        for h in parts:
            for way in range(2):
                far_c[way, step - 1, h].wait_recv()
                if step < 3 or h in held[way]:
                    far_c[way, step, h] = far_send(way, step, blocks[way], h)
        shares = [partial(blocks[way]) for way in range(2)]
        for h in parts:
            at = slice(h * span, (h + 1) * span)
            for way in range(2):
                share = shares[way][at]
                if (way, step - 1, h) in acc_c:
                    acc_c[way, step - 1, h].wait_recv()
                    share = share + acc_in[way, step - 1, at].astype(F32)
                acc_out[way, step, at] = share.astype(BF16)
                acc_c[way, step, h] = acc_send(way, step, h)
    for way in range(2):
        for h in held[way]:
            far_c[way, 3, h].wait_recv()
    def y_send(j):
        k = (j + Y - y) % Y
        return pltpu.make_async_remote_copy(
            src_ref=y_out.at[j], dst_ref=y_in.at[k], send_sem=ys_ss.at[k], recv_sem=ys_rs.at[k],
            device_id=device(z, j, l, x, core), device_id_type=MESH,
        )

    block = (home + Z // 2) % Z
    share = partial(block)
    for h in parts:
        at = slice(h * span, (h + 1) * span)
        for way in range(2):
            acc_c[way, 3, h].wait_recv()
        total = share[at] + acc_in[0, 3, at].astype(F32) + acc_in[1, 3, at].astype(F32)
        part[at] = total
        y_out[at] = total.astype(BF16)
        for j in range(h * span, (h + 1) * span):
            @pl.when(y != j)
            def _(j=j):
                y_send(j).start()

    total = part[y]
    for k in range(1, Y):
        pltpu.make_async_remote_copy(
            src_ref=y_out.at[0], dst_ref=y_in.at[k], send_sem=ys_ss.at[k], recv_sem=ys_rs.at[k],
            device_id=device(z, behind[k], l, x, core), device_id_type=MESH,
        ).wait_recv()
        total = total + y_in[k].astype(F32)
    mine = block * Y + y
    con[mine] = total.astype(BF16)
    def con_send(d, k):
        if d in (3, 4, 5):
            slot, to = (block + Z - d) % Z * Y + y, device(z, ahead[k], l, x, core)
        else:
            slot, to = block * Y + behind[k], plane[d]
        return send(con.at[slot], con.at[slot], con_ss.at[d, k], con_rs.at[d, k], to)

    def con_wait(d, k):
        con_c[d, k].wait_recv()
        settle((block + Z - d) % Z, behind[k] if k > 0 else y)

    def settle(b, j):
        con_f[place(b, j), :] = con[b * Y + j].astype(F32)

    con_c = {}
    for k in (2, 1, 3):
        con_c[0, k] = send(
            con.at[mine], con.at[mine], con_ss.at[0, k], con_rs.at[0, k], device(z, ahead[k], l, x, core))
    for d in (4, 3, 5, 2, 6, 1, 7):
        con_c[d, 0] = send(
            con.at[mine], con.at[mine], con_ss.at[d, 0], con_rs.at[d, 0], plane[d])
    settle(block, y)
    for step in ((0, 1), (0, 3), (3, 0), (5, 0), (0, 2), (4, 0)):
        d, k = step
        con_c[d, k].wait_recv()
        if d == 0:
            for e in (2, 6, 1, 7):
                con_c[e, k] = con_send(e, k)
        else:
            for e in (2, 1, 3):
                con_c[d, e] = con_send(d, e)
        settle((block + Z - d) % Z, behind[k] if k > 0 else y)
    for d in (1, 7, 2, 6):
        con_wait(d, 0)
    for k in (1, 3, 2):
        for d in (1, 7, 2, 6):
            con_wait(d, k)
    for d in (3, 5, 4):
        for k in (1, 3, 2):
            con_wait(d, k)
    load_interp.wait()
    con_m[...] = con_f[...].astype(BF16)

    def term(to, half):
        tile = interp[pl.ds(to * X, X), half]
        return jnp.dot(
            tile.reshape(-1, tile.shape[-1]), con_m[...], preferred_element_type=F32).reshape(X, *terms.shape[1:])

    order = ((1, 1 - l), (0, l))
    pair = {}
    for i, to in order:
        pair_out[i] = term(to, 1 - core).astype(BF16)
        pair[i] = send(pair_out.at[i], pair_in.at[i], pair_ss.at[i], pair_rs.at[i], sibling)
    fin = {}
    for i, to in order:
        both = term(to, core)
        pair[i].wait_recv()
        both = both + pair_in[i].astype(F32)
        fin_out[i] = both.astype(BF16)
        if i == 0:
            terms[...] = both
        for k in (2, 1, 3, 0):
            if (i, k) != (0, 0):
                fin[i, k] = send(
                    fin_out.at[i, (x + k) % X], fin_in.at[i, k], fin_ss.at[i * X + k], fin_rs.at[i * X + k],
                    device(z, y, (l + i) % L, (x + k) % X, core))
    total = terms[x]
    for i, k in fin:
        fin[i, k].wait_recv()
        total = total + fin_in[i, k].astype(F32)
    out[...] = total.astype(BF16)

    finish()


def local(orbitals, coulomb, interp):
    h, k = orbitals.shape
    m, n = coulomb.shape
    g = interp.shape[0]
    out = g // (L * X * C)
    dma = pltpu.SemaphoreType.DMA
    return pl.pallas_call(
        kernel,
        out_shape=jax.ShapeDtypeStruct((out, k), BF16),
        in_specs=[
            pl.BlockSpec(memory_space=pltpu.VMEM),
            pl.BlockSpec(memory_space=pltpu.HBM),
            pl.BlockSpec(memory_space=pltpu.HBM),
        ],
        out_specs=pl.BlockSpec(memory_space=pltpu.VMEM),
        scratch_shapes=[
            pltpu.VMEM((m, n), F32),
            pltpu.VMEM((n, m), F32),
            pltpu.VMEM((L * X, C, out, n), BF16),
            pltpu.VMEM((L * X * C, h, k), BF16),
            pltpu.VMEM((m, k), BF16),
            pltpu.VMEM((Z * Y, h, k), BF16),
            pltpu.VMEM((2, 4, Y, h, k), BF16),
            pltpu.VMEM((2, 4, Y, h, k), BF16),
            pltpu.VMEM((Y, h, k), F32),
            pltpu.VMEM((Y, h, k), BF16),
            pltpu.VMEM((Y, h, k), BF16),
            pltpu.VMEM((Z * Y, h, k), BF16),
            pltpu.VMEM((n, k), F32),
            pltpu.VMEM((n, k), BF16),
            pltpu.VMEM((h, k), BF16),
            pltpu.VMEM((X, out, k), F32),
            pltpu.VMEM((L, X, out, k), BF16),
            pltpu.VMEM((L, X, out, k), BF16),
            pltpu.VMEM((L, X, out, k), BF16),
            pltpu.VMEM((L, X, out, k), BF16),
            dma((2,)), dma((2,)), dma((8,)), dma((8,)), dma((8,)), dma((8,)), dma((4,)), dma((4,)),
            dma((2, 4, H)), dma((2, 4, H)), dma((2, 4, H)), dma((2, 4, H)), dma((4,)), dma((4,)),
            dma((Z, Y)), dma((Z, Y)), dma((2,)), dma((2,)), dma((8,)), dma((8,)),
        ],
        compiler_params=pltpu.CompilerParams(
            collective_id=0, has_side_effects=True, vmem_limit_bytes=62 * 1024 * 1024
        ),
        cost_estimate=pl.CostEstimate(
            flops=4 * m * n * k + 2 * g * n * k, bytes_accessed=4 * m * n + 2 * g * n, transcendentals=0
        ),
    )(orbitals, coulomb, interp.reshape(L * X, C, out, n))


def solution(mesh):
    in_specs = (P(("row", "col"), None), P("row", "col"), P("row", "col"))
    out_specs = P(("row", "col"), None)
    return jax.shard_map(local, mesh=mesh, in_specs=in_specs, out_specs=out_specs, check_vma=False)
```

```python
import jax
import jax.numpy as jnp
from jax import lax
from jax.experimental import pallas as pl
from jax.experimental.pallas import tpu as pltpu
from jax.sharding import PartitionSpec as P

MESH = pl.DeviceIdType.MESH
Z, Y, L, X, C = 8, 4, 2, 4, 2
F32, BF16 = jnp.float32, jnp.bfloat16
H = 4


def device(z, y, l, x, core):
    return (z * Y + y, (l * X + x) * C + core)


def mod(a, n):
    return a % n if isinstance(a, int) else lax.rem(a, n)


def div(a, n):
    return a // n if isinstance(a, int) else lax.div(a, n)


def side_of(turn):
    return mod(2 + X - div(turn, C), X)


def core_of(turn):
    return mod(turn + div(turn, X), C)


def turn_of(side, core):
    half = mod(2 + X - side, X)
    return half * C + mod(core + div(half, 2), C)


def rows(slots):
    n, h, k = slots.shape
    return slots.astype(F32).reshape(n * h, k)


def kernel(
    orb, coul_hbm, interp_hbm, out,
    coul, coul_t, interp, near_s, near, far, acc_in, acc_out, part,
    y_out, y_in, con, con_f, con_m, relay, terms, pair_out, pair_in, fin_out, fin_in,
    local_sem, relay_sem, near_ss, near_rs, sib_ss, sib_rs, perm_ss, perm_rs,
    far_ss, far_rs, acc_ss, acc_rs, ys_ss, ys_rs,
    con_ss, con_rs, pair_ss, pair_rs, fin_ss, fin_rs,
):
    row, col = lax.axis_index("row"), lax.axis_index("col")
    z, y = div(row, Y), mod(row, Y)
    l, x, core = div(col, X * C), mod(div(col, C), X), mod(col, C)
    up, down = device(mod(z + 1, Z), y, l, x, core), device(mod(z + Z - 1, Z), y, l, x, core)
    plane = [device(mod(z + d, Z), y, l, x, core) for d in range(Z)]
    sibling = device(z, y, l, x, 1 - core)
    chips = [None] + [(mod(l + k // X, L), mod(x + mod(k, X), X)) for k in range(1, L * X)]
    came = [None] + [(mod(l + k // X, L), mod(x + X - mod(k, X), X)) for k in range(1, L * X)]
    ahead = [None] + [mod(y + k, Y) for k in range(1, Y)]
    behind = [None] + [mod(y + Y - k, Y) for k in range(1, Y)]
    sends = []

    def send(src, dst, ss, rs, to):
        copy = pltpu.make_async_remote_copy(
            src_ref=src, dst_ref=dst, send_sem=ss, recv_sem=rs, device_id=to, device_id_type=MESH
        )
        copy.start()
        sends.append(copy)
        return copy

    home = mod(z + Z - div(col, C), Z)
    turn = turn_of(mod(x + X - mod(z, X), X), core)
    first_to = device(mod(z + turn, Z), y, l, mod(z, X), core)
    relayed = mod(z + Z - x, Z)
    other = jnp.where(core_of(relayed) == core, 0, 1)
    relayed = mod(relayed + other * X, Z)
    first_from = device(x + other * X, y, l, mod(x + side_of(relayed), X), core)
    piece = relayed * Y + (y % 2) * L + l
    targets = [device(z, mod(y + k, Y), other, x, div(y, 2)) for k in range(Y)]
    own_target = (other == l) & (div(y, 2) == core)
    sources = [device(z, core * 2 + j // L, mod(j, L), x, core_of(home)) for j in range(Y)]
    source_self = [(s[0] == row) & (s[1] == col) for s in sources]

    barrier = pltpu.get_barrier_semaphore()
    greet = [first_from] + [device(z, y, *chips[k], core) for k in range(1, L * X)] + [sibling] + plane[1:]
    greet += [device(z, ahead[k], l, x, core) for k in range(1, Y)]
    for d in greet:
        pl.semaphore_signal(barrier, inc=1, device_id=d, device_id_type=MESH)
    for j in range(Y):
        @pl.when(jnp.logical_not(source_self[j]))
        def _(j=j):
            pl.semaphore_signal(barrier, inc=1, device_id=sources[j], device_id_type=MESH)
    load_coul = pltpu.make_async_copy(coul_hbm, coul, local_sem.at[0])
    load_interp = pltpu.make_async_copy(interp_hbm, interp, local_sem.at[1])
    load_coul.start()
    load_interp.start()

    pl.semaphore_wait(barrier, jnp.where(own_target, len(greet) + Y - 1, len(greet) + Y))

    kind = mod(piece, Y)
    relay_c = send(orb, relay, relay_sem.at[0], relay_sem.at[1], first_to)

    def perm(j):
        return pltpu.make_async_remote_copy(
            src_ref=relay, dst_ref=far.at[piece], send_sem=perm_ss.at[j], recv_sem=perm_rs.at[kind],
            device_id=targets[j], device_id_type=MESH,
        )

    def finish():
        for c in sends:
            c.wait_send()
        for j in range(Y):
            @pl.when(y != j)
            def _(j=j):
                y_send(j).wait_send()
        for j in range(1, Y):
            perm(j).wait_send()

        @pl.when(jnp.logical_not(own_target))
        def _():
            perm(0).wait_send()

    near_s[col] = orb[...]
    sib = [send(orb, near_s.at[col], sib_ss.at[0], sib_rs.at[0], sibling)]
    near_c = [None]
    for k in range(1, L * X):
        near_c.append(send(orb, near_s.at[col], near_ss.at[k], near_rs.at[k], device(z, y, *chips[k], core)))

    relay_c.wait_recv()
    for j in (2, 1, 3):
        perm(j).start()

    @pl.when(jnp.logical_not(own_target))
    def _():
        perm(0).start()

    @pl.when(own_target)
    def _():
        far[piece] = relay[...]

    load_coul.wait()
    for k in range(coul.shape[1] // 128):
        coul_t[pl.ds(128 * k, 128), :] = coul[:, pl.ds(128 * k, 128)].T

    parts = range(H)
    span = Y // H
    held = (range(H // 2), range(H // 2, H))

    def far_send(way, step, block, h):
        at = pl.ds(block * Y + h * span, span)
        return send(far.at[at], far.at[at], far_ss.at[way, step, h], far_rs.at[way, step, h], (up, down)[way])

    def acc_send(way, step, h):
        at = pl.ds(h * span, span)
        return send(
            acc_out.at[way, step, at], acc_in.at[way, step, at],
            acc_ss.at[way, step, h], acc_rs.at[way, step, h], (up, down)[way])

    def place(block, j):
        n = orb.shape[0]
        p = (j // L) * (L * X * C) + (mod(j, L)) * (X * C) + (mod(x + side_of(block), X)) * C + core_of(block)
        return pl.ds(pl.multiple_of(p * n, n), n)

    def partial(block):
        points = rows(far[pl.ds(block * Y, Y)]).astype(BF16)
        density = lax.dot_general(points, near[...], (((1,), (1,)), ((), ())), preferred_element_type=F32)
        n = points.shape[0] // Y
        factor = jnp.concatenate([coul_t[place(block, j), :] for j in range(Y)], 0)
        weighted = (factor * density).astype(BF16)
        return jnp.dot(weighted, near[...], preferred_element_type=F32).reshape(Y, n, -1)

    far_c, acc_c = {}, {}
    for j in range(Y):
        @pl.when(jnp.logical_not(source_self[j]))
        def _(j=j):
            pltpu.make_async_remote_copy(
                src_ref=orb, dst_ref=far.at[home * Y + j], send_sem=perm_ss.at[j], recv_sem=perm_rs.at[j],
                device_id=sources[j], device_id_type=MESH,
            ).wait_recv()

        if (j + 1) % span == 0:
            for way in range(2):
                far_c[way, 0, j // span] = far_send(way, 0, home, j // span)
    for k in range(1, L * X):
        near_c[k].wait_recv()
        slot = (came[k][0] * X + came[k][1]) * C + core
        sib.append(send(near_s.at[slot], near_s.at[slot], sib_ss.at[k], sib_rs.at[k], sibling))

    for c in sib:
        c.wait_recv()
    near[...] = rows(near_s[...]).astype(BF16)

    own = partial(home)
    for way in range(2):
        for h in held[way]:
            at = slice(h * span, (h + 1) * span)
            acc_out[way, 0, at] = own[at].astype(BF16)
            acc_c[way, 0, h] = acc_send(way, 0, h)
    for step in range(1, 4):
        blocks = (mod(home + Z - step, Z), mod(home + step, Z))
        for h in parts:
            for way in range(2):
                far_c[way, step - 1, h].wait_recv()
                if step < 3 or h in held[way]:
                    far_c[way, step, h] = far_send(way, step, blocks[way], h)
        shares = [partial(blocks[way]) for way in range(2)]
        for h in parts:
            at = slice(h * span, (h + 1) * span)
            for way in range(2):
                share = shares[way][at]
                if (way, step - 1, h) in acc_c:
                    acc_c[way, step - 1, h].wait_recv()
                    share = share + acc_in[way, step - 1, at].astype(F32)
                acc_out[way, step, at] = share.astype(BF16)
                acc_c[way, step, h] = acc_send(way, step, h)
    for way in range(2):
        for h in held[way]:
            far_c[way, 3, h].wait_recv()
    def y_send(j):
        k = mod(j + Y - y, Y)
        return pltpu.make_async_remote_copy(
            src_ref=y_out.at[j], dst_ref=y_in.at[k], send_sem=ys_ss.at[k], recv_sem=ys_rs.at[k],
            device_id=device(z, j, l, x, core), device_id_type=MESH,
        )

    block = mod(home + Z // 2, Z)
    share = partial(block)
    for h in parts:
        at = slice(h * span, (h + 1) * span)
        for way in range(2):
            acc_c[way, 3, h].wait_recv()
        total = share[at] + acc_in[0, 3, at].astype(F32) + acc_in[1, 3, at].astype(F32)
        part[at] = total
        y_out[at] = total.astype(BF16)
        for j in range(h * span, (h + 1) * span):
            @pl.when(y != j)
            def _(j=j):
                y_send(j).start()

    total = part[y]
    for k in range(1, Y):
        pltpu.make_async_remote_copy(
            src_ref=y_out.at[0], dst_ref=y_in.at[k], send_sem=ys_ss.at[k], recv_sem=ys_rs.at[k],
            device_id=device(z, behind[k], l, x, core), device_id_type=MESH,
        ).wait_recv()
        total = total + y_in[k].astype(F32)
    mine = block * Y + y
    con[mine] = total.astype(BF16)
    def con_send(d, k):
        if d in (3, 4, 5):
            slot, to = mod(block + Z - d, Z) * Y + y, device(z, ahead[k], l, x, core)
        else:
            slot, to = block * Y + behind[k], plane[d]
        return send(con.at[slot], con.at[slot], con_ss.at[d, k], con_rs.at[d, k], to)

    def con_wait(d, k):
        con_c[d, k].wait_recv()
        settle(mod(block + Z - d, Z), behind[k] if k > 0 else y)

    def settle(b, j):
        con_f[place(b, j), :] = con[b * Y + j].astype(F32)

    con_c = {}
    for k in (2, 1, 3):
        con_c[0, k] = send(
            con.at[mine], con.at[mine], con_ss.at[0, k], con_rs.at[0, k], device(z, ahead[k], l, x, core))
    for d in (4, 3, 5, 2, 6, 1, 7):
        con_c[d, 0] = send(
            con.at[mine], con.at[mine], con_ss.at[d, 0], con_rs.at[d, 0], plane[d])
    settle(block, y)
    for step in ((0, 1), (0, 3), (3, 0), (5, 0), (0, 2), (4, 0)):
        d, k = step
        con_c[d, k].wait_recv()
        if d == 0:
            for e in (2, 6, 1, 7):
                con_c[e, k] = con_send(e, k)
        else:
            for e in (2, 1, 3):
                con_c[d, e] = con_send(d, e)
        settle(mod(block + Z - d, Z), behind[k] if k > 0 else y)
    for d in (1, 7, 2, 6):
        con_wait(d, 0)
    for k in (1, 3, 2):
        for d in (1, 7, 2, 6):
            con_wait(d, k)
    for d in (3, 5, 4):
        for k in (1, 3, 2):
            con_wait(d, k)
    load_interp.wait()
    con_m[...] = con_f[...].astype(BF16)

    def term(to, half):
        tile = interp[pl.ds(to * X, X), half]
        return jnp.dot(
            tile.reshape(-1, tile.shape[-1]), con_m[...], preferred_element_type=F32).reshape(X, *terms.shape[1:])

    order = ((1, 1 - l), (0, l))
    pair = {}
    for i, to in order:
        pair_out[i] = term(to, 1 - core).astype(BF16)
        pair[i] = send(pair_out.at[i], pair_in.at[i], pair_ss.at[i], pair_rs.at[i], sibling)
    fin = {}
    for i, to in order:
        both = term(to, core)
        pair[i].wait_recv()
        both = both + pair_in[i].astype(F32)
        fin_out[i] = both.astype(BF16)
        if i == 0:
            terms[...] = both
        for k in (2, 1, 3, 0):
            if (i, k) != (0, 0):
                fin[i, k] = send(
                    fin_out.at[i, mod(x + k, X)], fin_in.at[i, k], fin_ss.at[i * X + k], fin_rs.at[i * X + k],
                    device(z, y, mod(l + i, L), mod(x + k, X), core))
    total = terms[x]
    for i, k in fin:
        fin[i, k].wait_recv()
        total = total + fin_in[i, k].astype(F32)
    out[...] = total.astype(BF16)

    finish()


def local(orbitals, coulomb, interp):
    h, k = orbitals.shape
    m, n = coulomb.shape
    g = interp.shape[0]
    out = g // (L * X * C)
    dma = pltpu.SemaphoreType.DMA
    return pl.pallas_call(
        kernel,
        out_shape=jax.ShapeDtypeStruct((out, k), BF16),
        in_specs=[
            pl.BlockSpec(memory_space=pltpu.VMEM),
            pl.BlockSpec(memory_space=pltpu.HBM),
            pl.BlockSpec(memory_space=pltpu.HBM),
        ],
        out_specs=pl.BlockSpec(memory_space=pltpu.VMEM),
        scratch_shapes=[
            pltpu.VMEM((m, n), F32),
            pltpu.VMEM((n, m), F32),
            pltpu.VMEM((L * X, C, out, n), BF16),
            pltpu.VMEM((L * X * C, h, k), BF16),
            pltpu.VMEM((m, k), BF16),
            pltpu.VMEM((Z * Y, h, k), BF16),
            pltpu.VMEM((2, 4, Y, h, k), BF16),
            pltpu.VMEM((2, 4, Y, h, k), BF16),
            pltpu.VMEM((Y, h, k), F32),
            pltpu.VMEM((Y, h, k), BF16),
            pltpu.VMEM((Y, h, k), BF16),
            pltpu.VMEM((Z * Y, h, k), BF16),
            pltpu.VMEM((n, k), F32),
            pltpu.VMEM((n, k), BF16),
            pltpu.VMEM((h, k), BF16),
            pltpu.VMEM((X, out, k), F32),
            pltpu.VMEM((L, X, out, k), BF16),
            pltpu.VMEM((L, X, out, k), BF16),
            pltpu.VMEM((L, X, out, k), BF16),
            pltpu.VMEM((L, X, out, k), BF16),
            dma((2,)), dma((2,)), dma((8,)), dma((8,)), dma((8,)), dma((8,)), dma((4,)), dma((4,)),
            dma((2, 4, H)), dma((2, 4, H)), dma((2, 4, H)), dma((2, 4, H)), dma((4,)), dma((4,)),
            dma((Z, Y)), dma((Z, Y)), dma((2,)), dma((2,)), dma((8,)), dma((8,)),
        ],
        compiler_params=pltpu.CompilerParams(
            collective_id=0, has_side_effects=True, vmem_limit_bytes=62 * 1024 * 1024
        ),
        cost_estimate=pl.CostEstimate(
            flops=4 * m * n * k + 2 * g * n * k, bytes_accessed=4 * m * n + 2 * g * n, transcendentals=0
        ),
    )(orbitals, coulomb, interp.reshape(L * X, C, out, n))


def solution(mesh):
    in_specs = (P(("row", "col"), None), P("row", "col"), P("row", "col"))
    out_specs = P(("row", "col"), None)
    return jax.shard_map(local, mesh=mesh, in_specs=in_specs, out_specs=out_specs, check_vma=False)
```

```python
import jax
import jax.numpy as jnp
from jax import lax
from jax.experimental import pallas as pl
from jax.experimental.pallas import tpu as pltpu
from jax.sharding import PartitionSpec as P

MESH = pl.DeviceIdType.MESH
Z, Y, L, X, C = 8, 4, 2, 4, 2
F32, BF16 = jnp.float32, jnp.bfloat16
H = 4


def device(z, y, l, x, core):
    return (z * Y + y, (l * X + x) * C + core)


def mod(a, n):
    return a % n if isinstance(a, int) else lax.rem(a, n)


def div(a, n):
    return a // n if isinstance(a, int) else lax.div(a, n)


def side_of(turn):
    return mod(2 + X - div(turn, C), X)


def core_of(turn):
    return mod(turn + div(turn, X), C)


def turn_of(side, core):
    half = mod(2 + X - side, X)
    return half * C + mod(core + div(half, 2), C)


def rows(slots):
    n, h, k = slots.shape
    return slots.astype(F32).reshape(n * h, k)


def kernel(
    orb, coul_hbm, interp_hbm, out,
    coul, coul_t, interp, near_s, near, far, acc_in, acc_out, part,
    y_out, y_in, con, con_f, con_m, relay, terms, pair_out, pair_in, fin_out, fin_in,
    local_sem, relay_sem, near_ss, near_rs, sib_ss, sib_rs, perm_ss, perm_rs,
    far_ss, far_rs, acc_ss, acc_rs, ys_ss, ys_rs,
    con_ss, con_rs, pair_ss, pair_rs, fin_ss, fin_rs,
):
    row, col = lax.axis_index("row"), lax.axis_index("col")
    z, y = div(row, Y), mod(row, Y)
    l, x, core = div(col, X * C), mod(div(col, C), X), mod(col, C)
    up, down = device(mod(z + 1, Z), y, l, x, core), device(mod(z + Z - 1, Z), y, l, x, core)
    plane = [device(mod(z + d, Z), y, l, x, core) for d in range(Z)]
    sibling = device(z, y, l, x, 1 - core)
    chips = [None] + [(mod(l + k // X, L), mod(x + mod(k, X), X)) for k in range(1, L * X)]
    came = [None] + [(mod(l + k // X, L), mod(x + X - mod(k, X), X)) for k in range(1, L * X)]
    ahead = [None] + [mod(y + k, Y) for k in range(1, Y)]
    behind = [None] + [mod(y + Y - k, Y) for k in range(1, Y)]
    sends = []

    def send(src, dst, ss, rs, to):
        copy = pltpu.make_async_remote_copy(
            src_ref=src, dst_ref=dst, send_sem=ss, recv_sem=rs, device_id=to, device_id_type=MESH
        )
        copy.start()
        sends.append(copy)
        return copy

    home = mod(z + Z - div(col, C), Z)
    turn = turn_of(mod(x + X - mod(z, X), X), core)
    first_to = device(mod(z + turn, Z), y, l, mod(z, X), core)
    relayed = mod(z + Z - x, Z)
    other = jnp.where(core_of(relayed) == core, 0, 1)
    relayed = mod(relayed + other * X, Z)
    first_from = device(x + other * X, y, l, mod(x + side_of(relayed), X), core)
    piece = relayed * Y + (y % 2) * L + l
    targets = [device(z, mod(y + k, Y), other, x, div(y, 2)) for k in range(Y)]
    own_target = (other == l) & (div(y, 2) == core)
    sources = [device(z, core * 2 + j // L, mod(j, L), x, core_of(home)) for j in range(Y)]
    source_self = [(s[0] == row) & (s[1] == col) for s in sources]

    barrier = pltpu.get_barrier_semaphore()
    greet = [first_from] + [device(z, y, *chips[k], core) for k in range(1, L * X)] + [sibling] + plane[1:]
    greet += [device(z, ahead[k], l, x, core) for k in range(1, Y)]
    for d in greet:
        pl.semaphore_signal(barrier, inc=1, device_id=d, device_id_type=MESH)
    for j in range(Y):
        @pl.when(jnp.logical_not(source_self[j]))
        def _(j=j):
            pl.semaphore_signal(barrier, inc=1, device_id=sources[j], device_id_type=MESH)
    load_coul = pltpu.make_async_copy(coul_hbm, coul, local_sem.at[0])
    load_interp = pltpu.make_async_copy(interp_hbm, interp, local_sem.at[1])
    load_coul.start()
    load_interp.start()

    pl.semaphore_wait(barrier, jnp.where(own_target, len(greet) + Y - 1, len(greet) + Y))

    kind = mod(piece, Y)
    relay_c = send(orb, relay, relay_sem.at[0], relay_sem.at[1], first_to)

    def perm(j):
        return pltpu.make_async_remote_copy(
            src_ref=relay, dst_ref=far.at[piece], send_sem=perm_ss.at[j], recv_sem=perm_rs.at[kind],
            device_id=targets[j], device_id_type=MESH,
        )

    def finish():
        for c in sends:
            c.wait_send()
        for j in range(Y):
            @pl.when(y != j)
            def _(j=j):
                y_send(j).wait_send()
        for j in range(1, Y):
            perm(j).wait_send()

        @pl.when(jnp.logical_not(own_target))
        def _():
            perm(0).wait_send()

    near_s[col] = orb[...]
    sib = [send(orb, near_s.at[col], sib_ss.at[0], sib_rs.at[0], sibling)]
    near_c = [None]
    for k in range(1, L * X):
        near_c.append(send(orb, near_s.at[col], near_ss.at[k], near_rs.at[k], device(z, y, *chips[k], core)))

    relay_c.wait_recv()
    for j in (2, 1, 3):
        perm(j).start()

    @pl.when(jnp.logical_not(own_target))
    def _():
        perm(0).start()

    @pl.when(own_target)
    def _():
        far[piece] = relay[...]

    load_coul.wait()
    for k in range(coul.shape[1] // 128):
        coul_t[pl.ds(128 * k, 128), :] = coul[:, pl.ds(128 * k, 128)].T

    parts = range(H)
    span = Y // H
    held = (range(H // 2), range(H // 2, H))

    def far_send(way, step, block, h):
        at = pl.ds(block * Y + h * span, span)
        return send(far.at[at], far.at[at], far_ss.at[way, step, h], far_rs.at[way, step, h], (up, down)[way])

    def acc_send(way, step, h):
        at = pl.ds(h * span, span)
        return send(
            acc_out.at[way, step, at], acc_in.at[way, step, at],
            acc_ss.at[way, step, h], acc_rs.at[way, step, h], (up, down)[way])

    def place(block, j):
        n = orb.shape[0]
        p = (j // L) * (L * X * C) + (mod(j, L)) * (X * C) + (mod(x + side_of(block), X)) * C + core_of(block)
        return pl.ds(pl.multiple_of(p * n, n), n)

    def partial(block):
        points = rows(far[pl.ds(block * Y, Y)]).astype(BF16)
        density = lax.dot_general(points, near[...], (((1,), (1,)), ((), ())), preferred_element_type=F32)
        n = points.shape[0] // Y
        factor = jnp.concatenate([coul_t[place(block, j), :] for j in range(Y)], 0)
        weighted = (factor * density).astype(BF16)
        return jnp.dot(weighted, near[...], preferred_element_type=F32).reshape(Y, n, -1)

    far_c, acc_c = {}, {}
    for j in range(Y):
        @pl.when(jnp.logical_not(source_self[j]))
        def _(j=j):
            pltpu.make_async_remote_copy(
                src_ref=orb, dst_ref=far.at[home * Y + j], send_sem=perm_ss.at[j], recv_sem=perm_rs.at[j],
                device_id=sources[j], device_id_type=MESH,
            ).wait_recv()

        if (j + 1) % span == 0:
            for way in range(2):
                far_c[way, 0, j // span] = far_send(way, 0, home, j // span)
    for k in range(1, L * X):
        near_c[k].wait_recv()
        slot = (came[k][0] * X + came[k][1]) * C + core
        sib.append(send(near_s.at[slot], near_s.at[slot], sib_ss.at[k], sib_rs.at[k], sibling))

    for c in sib:
        c.wait_recv()
    near[...] = rows(near_s[...]).astype(BF16)

    own = partial(home)
    for way in range(2):
        for h in held[way]:
            at = slice(h * span, (h + 1) * span)
            acc_out[way, 0, at] = own[at].astype(BF16)
            acc_c[way, 0, h] = acc_send(way, 0, h)
    for step in range(1, 4):
        blocks = (mod(home + Z - step, Z), mod(home + step, Z))
        for h in parts:
            for way in range(2):
                far_c[way, step - 1, h].wait_recv()
                if step < 3 or h in held[way]:
                    far_c[way, step, h] = far_send(way, step, blocks[way], h)
        shares = [partial(blocks[way]) for way in range(2)]
        for h in parts:
            at = slice(h * span, (h + 1) * span)
            for way in range(2):
                share = shares[way][at]
                if (way, step - 1, h) in acc_c:
                    acc_c[way, step - 1, h].wait_recv()
                    share = share + acc_in[way, step - 1, at].astype(F32)
                acc_out[way, step, at] = share.astype(BF16)
                acc_c[way, step, h] = acc_send(way, step, h)
    for way in range(2):
        for h in held[way]:
            far_c[way, 3, h].wait_recv()
    def y_send(j):
        k = mod(j + Y - y, Y)
        return pltpu.make_async_remote_copy(
            src_ref=y_out.at[j], dst_ref=y_in.at[k], send_sem=ys_ss.at[k], recv_sem=ys_rs.at[k],
            device_id=device(z, j, l, x, core), device_id_type=MESH,
        )

    block = mod(home + Z // 2, Z)
    share = partial(block)
    for h in parts:
        at = slice(h * span, (h + 1) * span)
        for way in range(2):
            acc_c[way, 3, h].wait_recv()
        total = share[at] + acc_in[0, 3, at].astype(F32) + acc_in[1, 3, at].astype(F32)
        part[at] = total
        y_out[at] = total.astype(BF16)
        for j in range(h * span, (h + 1) * span):
            @pl.when(y != j)
            def _(j=j):
                y_send(j).start()

    total = part[y]
    for k in range(1, Y):
        pltpu.make_async_remote_copy(
            src_ref=y_out.at[0], dst_ref=y_in.at[k], send_sem=ys_ss.at[k], recv_sem=ys_rs.at[k],
            device_id=device(z, behind[k], l, x, core), device_id_type=MESH,
        ).wait_recv()
        total = total + y_in[k].astype(F32)
    mine = block * Y + y
    con[mine] = total.astype(BF16)
    def con_send(d, k):
        if d in (3, 4, 5):
            slot, to = mod(block + Z - d, Z) * Y + y, device(z, ahead[k], l, x, core)
        else:
            slot, to = block * Y + behind[k], plane[d]
        return send(con.at[slot], con.at[slot], con_ss.at[d, k], con_rs.at[d, k], to)

    def con_wait(d, k):
        con_c[d, k].wait_recv()
        settle(mod(block + Z - d, Z), behind[k] if k > 0 else y)

    def settle(b, j):
        con_f[place(b, j), :] = con[b * Y + j].astype(F32)

    con_c = {}
    for k in (2, 1, 3):
        con_c[0, k] = send(
            con.at[mine], con.at[mine], con_ss.at[0, k], con_rs.at[0, k], device(z, ahead[k], l, x, core))
    for d in (4, 3, 5, 2, 6, 1, 7):
        con_c[d, 0] = send(
            con.at[mine], con.at[mine], con_ss.at[d, 0], con_rs.at[d, 0], plane[d])
    settle(block, y)
    for step in ((0, 1), (0, 3), (3, 0), (5, 0), (4, 0), (0, 2)):
        d, k = step
        con_c[d, k].wait_recv()
        if d == 0:
            for e in (2, 6, 1, 7):
                con_c[e, k] = con_send(e, k)
        else:
            for e in (2, 1, 3):
                con_c[d, e] = con_send(d, e)
        settle(mod(block + Z - d, Z), behind[k] if k > 0 else y)
    for d in (1, 7, 2, 6):
        con_wait(d, 0)
    for k in (1, 3, 2):
        for d in (1, 7, 2, 6):
            con_wait(d, k)
    for d in (3, 5, 4):
        for k in (1, 3, 2):
            con_wait(d, k)
    load_interp.wait()
    con_m[...] = con_f[...].astype(BF16)

    def term(to, half):
        tile = interp[pl.ds(to * X, X), half]
        return jnp.dot(
            tile.reshape(-1, tile.shape[-1]), con_m[...], preferred_element_type=F32).reshape(X, *terms.shape[1:])

    order = ((1, 1 - l), (0, l))
    pair = {}
    for i, to in order:
        pair_out[i] = term(to, 1 - core).astype(BF16)
        pair[i] = send(pair_out.at[i], pair_in.at[i], pair_ss.at[i], pair_rs.at[i], sibling)
    fin = {}
    for i, to in order:
        both = term(to, core)
        pair[i].wait_recv()
        both = both + pair_in[i].astype(F32)
        fin_out[i] = both.astype(BF16)
        if i == 0:
            terms[...] = both
        for k in (2, 1, 3, 0):
            if (i, k) != (0, 0):
                fin[i, k] = send(
                    fin_out.at[i, mod(x + k, X)], fin_in.at[i, k], fin_ss.at[i * X + k], fin_rs.at[i * X + k],
                    device(z, y, mod(l + i, L), mod(x + k, X), core))
    total = terms[x]
    for i, k in fin:
        fin[i, k].wait_recv()
        total = total + fin_in[i, k].astype(F32)
    out[...] = total.astype(BF16)

    finish()


def local(orbitals, coulomb, interp):
    h, k = orbitals.shape
    m, n = coulomb.shape
    g = interp.shape[0]
    out = g // (L * X * C)
    dma = pltpu.SemaphoreType.DMA
    return pl.pallas_call(
        kernel,
        out_shape=jax.ShapeDtypeStruct((out, k), BF16),
        in_specs=[
            pl.BlockSpec(memory_space=pltpu.VMEM),
            pl.BlockSpec(memory_space=pltpu.HBM),
            pl.BlockSpec(memory_space=pltpu.HBM),
        ],
        out_specs=pl.BlockSpec(memory_space=pltpu.VMEM),
        scratch_shapes=[
            pltpu.VMEM((m, n), F32),
            pltpu.VMEM((n, m), F32),
            pltpu.VMEM((L * X, C, out, n), BF16),
            pltpu.VMEM((L * X * C, h, k), BF16),
            pltpu.VMEM((m, k), BF16),
            pltpu.VMEM((Z * Y, h, k), BF16),
            pltpu.VMEM((2, 4, Y, h, k), BF16),
            pltpu.VMEM((2, 4, Y, h, k), BF16),
            pltpu.VMEM((Y, h, k), F32),
            pltpu.VMEM((Y, h, k), BF16),
            pltpu.VMEM((Y, h, k), BF16),
            pltpu.VMEM((Z * Y, h, k), BF16),
            pltpu.VMEM((n, k), F32),
            pltpu.VMEM((n, k), BF16),
            pltpu.VMEM((h, k), BF16),
            pltpu.VMEM((X, out, k), F32),
            pltpu.VMEM((L, X, out, k), BF16),
            pltpu.VMEM((L, X, out, k), BF16),
            pltpu.VMEM((L, X, out, k), BF16),
            pltpu.VMEM((L, X, out, k), BF16),
            dma((2,)), dma((2,)), dma((8,)), dma((8,)), dma((8,)), dma((8,)), dma((4,)), dma((4,)),
            dma((2, 4, H)), dma((2, 4, H)), dma((2, 4, H)), dma((2, 4, H)), dma((4,)), dma((4,)),
            dma((Z, Y)), dma((Z, Y)), dma((2,)), dma((2,)), dma((8,)), dma((8,)),
        ],
        compiler_params=pltpu.CompilerParams(
            collective_id=0, has_side_effects=True, vmem_limit_bytes=62 * 1024 * 1024
        ),
        cost_estimate=pl.CostEstimate(
            flops=4 * m * n * k + 2 * g * n * k, bytes_accessed=4 * m * n + 2 * g * n, transcendentals=0
        ),
    )(orbitals, coulomb, interp.reshape(L * X, C, out, n))


def solution(mesh):
    in_specs = (P(("row", "col"), None), P("row", "col"), P("row", "col"))
    out_specs = P(("row", "col"), None)
    return jax.shard_map(local, mesh=mesh, in_specs=in_specs, out_specs=out_specs, check_vma=False)
```

```python
import jax
import jax.numpy as jnp
from jax import lax
from jax.experimental import pallas as pl
from jax.experimental.pallas import tpu as pltpu
from jax.sharding import PartitionSpec as P

MESH = pl.DeviceIdType.MESH
Z, Y, L, X, C = 8, 4, 2, 4, 2
F32, BF16 = jnp.float32, jnp.bfloat16
H = 2


def device(z, y, l, x, core):
    return (z * Y + y, (l * X + x) * C + core)


def mod(a, n):
    return a % n if isinstance(a, int) else lax.rem(a, n)


def div(a, n):
    return a // n if isinstance(a, int) else lax.div(a, n)


def side_of(turn):
    return mod(2 + X - div(turn, C), X)


def core_of(turn):
    return mod(turn + div(turn, X), C)


def turn_of(side, core):
    half = mod(2 + X - side, X)
    return half * C + mod(core + div(half, 2), C)


def rows(slots):
    n, h, k = slots.shape
    return slots.astype(F32).reshape(n * h, k)


def kernel(
    orb, coul_hbm, interp_hbm, out,
    coul, coul_t, interp, near_s, near, far, acc_in, acc_out, part,
    y_out, y_in, con, con_f, con_m, relay, terms, pair_out, pair_in, fin_out, fin_in,
    local_sem, relay_sem, near_ss, near_rs, sib_ss, sib_rs, perm_ss, perm_rs,
    far_ss, far_rs, acc_ss, acc_rs, ys_ss, ys_rs,
    con_ss, con_rs, pair_ss, pair_rs, fin_ss, fin_rs,
):
    row, col = lax.axis_index("row"), lax.axis_index("col")
    z, y = div(row, Y), mod(row, Y)
    l, x, core = div(col, X * C), mod(div(col, C), X), mod(col, C)
    up, down = device(mod(z + 1, Z), y, l, x, core), device(mod(z + Z - 1, Z), y, l, x, core)
    plane = [device(mod(z + d, Z), y, l, x, core) for d in range(Z)]
    sibling = device(z, y, l, x, 1 - core)
    chips = [None] + [(mod(l + k // X, L), mod(x + mod(k, X), X)) for k in range(1, L * X)]
    came = [None] + [(mod(l + k // X, L), mod(x + X - mod(k, X), X)) for k in range(1, L * X)]
    ahead = [None] + [mod(y + k, Y) for k in range(1, Y)]
    behind = [None] + [mod(y + Y - k, Y) for k in range(1, Y)]
    sends = []

    def send(src, dst, ss, rs, to):
        copy = pltpu.make_async_remote_copy(
            src_ref=src, dst_ref=dst, send_sem=ss, recv_sem=rs, device_id=to, device_id_type=MESH
        )
        copy.start()
        sends.append(copy)
        return copy

    home = mod(z + Z - div(col, C), Z)
    turn = turn_of(mod(x + X - mod(z, X), X), core)
    first_to = device(mod(z + turn, Z), y, l, mod(z, X), core)
    relayed = mod(z + Z - x, Z)
    other = jnp.where(core_of(relayed) == core, 0, 1)
    relayed = mod(relayed + other * X, Z)
    first_from = device(x + other * X, y, l, mod(x + side_of(relayed), X), core)
    piece = relayed * Y + (y % 2) * L + l
    targets = [device(z, mod(y + k, Y), other, x, div(y, 2)) for k in range(Y)]
    own_target = (other == l) & (div(y, 2) == core)
    sources = [device(z, core * 2 + j // L, mod(j, L), x, core_of(home)) for j in range(Y)]
    source_self = [(s[0] == row) & (s[1] == col) for s in sources]

    barrier = pltpu.get_barrier_semaphore()
    greet = [first_from] + [device(z, y, *chips[k], core) for k in range(1, L * X)] + [sibling] + plane[1:]
    greet += [device(z, ahead[k], l, x, core) for k in range(1, Y)]
    for d in greet:
        pl.semaphore_signal(barrier, inc=1, device_id=d, device_id_type=MESH)
    for j in range(Y):
        @pl.when(jnp.logical_not(source_self[j]))
        def _(j=j):
            pl.semaphore_signal(barrier, inc=1, device_id=sources[j], device_id_type=MESH)
    load_coul = pltpu.make_async_copy(coul_hbm, coul, local_sem.at[0])
    load_interp = pltpu.make_async_copy(interp_hbm, interp, local_sem.at[1])
    load_coul.start()
    load_interp.start()

    pl.semaphore_wait(barrier, jnp.where(own_target, len(greet) + Y - 1, len(greet) + Y))

    kind = mod(piece, Y)
    relay_c = send(orb, relay, relay_sem.at[0], relay_sem.at[1], first_to)

    def perm(j):
        return pltpu.make_async_remote_copy(
            src_ref=relay, dst_ref=far.at[piece], send_sem=perm_ss.at[j], recv_sem=perm_rs.at[kind],
            device_id=targets[j], device_id_type=MESH,
        )

    def finish():
        for c in sends:
            c.wait_send()
        for j in range(Y):
            @pl.when(y != j)
            def _(j=j):
                y_send(j).wait_send()
        for j in range(1, Y):
            perm(j).wait_send()

        @pl.when(jnp.logical_not(own_target))
        def _():
            perm(0).wait_send()

    near_s[col] = orb[...]
    sib = [send(orb, near_s.at[col], sib_ss.at[0], sib_rs.at[0], sibling)]
    near_c = [None]
    for k in range(1, L * X):
        near_c.append(send(orb, near_s.at[col], near_ss.at[k], near_rs.at[k], device(z, y, *chips[k], core)))

    relay_c.wait_recv()
    for j in (2, 1, 3):
        perm(j).start()

    @pl.when(jnp.logical_not(own_target))
    def _():
        perm(0).start()

    @pl.when(own_target)
    def _():
        far[piece] = relay[...]

    load_coul.wait()
    for k in range(coul.shape[1] // 128):
        coul_t[pl.ds(128 * k, 128), :] = coul[:, pl.ds(128 * k, 128)].T

    parts = range(H)
    span = Y // H
    held = (range(H // 2), range(H // 2, H))

    def far_send(way, step, block, h):
        at = pl.ds(block * Y + h * span, span)
        return send(far.at[at], far.at[at], far_ss.at[way, step, h], far_rs.at[way, step, h], (up, down)[way])

    def acc_send(way, step, h):
        at = pl.ds(h * span, span)
        return send(
            acc_out.at[way, step, at], acc_in.at[way, step, at],
            acc_ss.at[way, step, h], acc_rs.at[way, step, h], (up, down)[way])

    def place(block, j):
        n = orb.shape[0]
        p = (j // L) * (L * X * C) + (mod(j, L)) * (X * C) + (mod(x + side_of(block), X)) * C + core_of(block)
        return pl.ds(pl.multiple_of(p * n, n), n)

    def partial(block):
        points = rows(far[pl.ds(block * Y, Y)]).astype(BF16)
        density = lax.dot_general(points, near[...], (((1,), (1,)), ((), ())), preferred_element_type=F32)
        n = points.shape[0] // Y
        factor = jnp.concatenate([coul_t[place(block, j), :] for j in range(Y)], 0)
        weighted = (factor * density).astype(BF16)
        return jnp.dot(weighted, near[...], preferred_element_type=F32).reshape(Y, n, -1)

    far_c, acc_c = {}, {}
    for j in range(Y):
        @pl.when(jnp.logical_not(source_self[j]))
        def _(j=j):
            pltpu.make_async_remote_copy(
                src_ref=orb, dst_ref=far.at[home * Y + j], send_sem=perm_ss.at[j], recv_sem=perm_rs.at[j],
                device_id=sources[j], device_id_type=MESH,
            ).wait_recv()

        if (j + 1) % span == 0:
            for way in range(2):
                far_c[way, 0, j // span] = far_send(way, 0, home, j // span)
    for k in range(1, L * X):
        near_c[k].wait_recv()
        slot = (came[k][0] * X + came[k][1]) * C + core
        sib.append(send(near_s.at[slot], near_s.at[slot], sib_ss.at[k], sib_rs.at[k], sibling))

    for c in sib:
        c.wait_recv()
    near[...] = rows(near_s[...]).astype(BF16)

    own = partial(home)
    for way in range(2):
        for h in held[way]:
            at = slice(h * span, (h + 1) * span)
            acc_out[way, 0, at] = own[at].astype(BF16)
            acc_c[way, 0, h] = acc_send(way, 0, h)
    for step in range(1, 4):
        blocks = (mod(home + Z - step, Z), mod(home + step, Z))
        for h in parts:
            for way in range(2):
                far_c[way, step - 1, h].wait_recv()
                if step < 3 or h in held[way]:
                    far_c[way, step, h] = far_send(way, step, blocks[way], h)
        shares = [partial(blocks[way]) for way in range(2)]
        for h in parts:
            at = slice(h * span, (h + 1) * span)
            for way in range(2):
                share = shares[way][at]
                if (way, step - 1, h) in acc_c:
                    acc_c[way, step - 1, h].wait_recv()
                    share = share + acc_in[way, step - 1, at].astype(F32)
                acc_out[way, step, at] = share.astype(BF16)
                acc_c[way, step, h] = acc_send(way, step, h)
    for way in range(2):
        for h in held[way]:
            far_c[way, 3, h].wait_recv()
    def y_send(j):
        k = mod(j + Y - y, Y)
        return pltpu.make_async_remote_copy(
            src_ref=y_out.at[j], dst_ref=y_in.at[k], send_sem=ys_ss.at[k], recv_sem=ys_rs.at[k],
            device_id=device(z, j, l, x, core), device_id_type=MESH,
        )

    block = mod(home + Z // 2, Z)
    share = partial(block)
    for h in parts:
        at = slice(h * span, (h + 1) * span)
        for way in range(2):
            acc_c[way, 3, h].wait_recv()
        total = share[at] + acc_in[0, 3, at].astype(F32) + acc_in[1, 3, at].astype(F32)
        part[at] = total
        y_out[at] = total.astype(BF16)
        for j in range(h * span, (h + 1) * span):
            @pl.when(y != j)
            def _(j=j):
                y_send(j).start()

    total = part[y]
    for k in range(1, Y):
        pltpu.make_async_remote_copy(
            src_ref=y_out.at[0], dst_ref=y_in.at[k], send_sem=ys_ss.at[k], recv_sem=ys_rs.at[k],
            device_id=device(z, behind[k], l, x, core), device_id_type=MESH,
        ).wait_recv()
        total = total + y_in[k].astype(F32)
    mine = block * Y + y
    con[mine] = total.astype(BF16)
    def con_send(d, k):
        if d in (3, 4, 5):
            slot, to = mod(block + Z - d, Z) * Y + y, device(z, ahead[k], l, x, core)
        else:
            slot, to = block * Y + behind[k], plane[d]
        return send(con.at[slot], con.at[slot], con_ss.at[d, k], con_rs.at[d, k], to)

    def con_wait(d, k):
        con_c[d, k].wait_recv()
        settle(mod(block + Z - d, Z), behind[k] if k > 0 else y)

    def settle(b, j):
        con_f[place(b, j), :] = con[b * Y + j].astype(F32)

    con_c = {}
    for k in (2, 1, 3):
        con_c[0, k] = send(
            con.at[mine], con.at[mine], con_ss.at[0, k], con_rs.at[0, k], device(z, ahead[k], l, x, core))
    for d in (4, 3, 5, 2, 6, 1, 7):
        con_c[d, 0] = send(
            con.at[mine], con.at[mine], con_ss.at[d, 0], con_rs.at[d, 0], plane[d])
    settle(block, y)
    for step in ((0, 1), (0, 3), (3, 0), (5, 0), (0, 2), (4, 0)):
        d, k = step
        con_c[d, k].wait_recv()
        if d == 0:
            for e in (2, 6, 1, 7):
                con_c[e, k] = con_send(e, k)
        else:
            for e in (2, 1, 3):
                con_c[d, e] = con_send(d, e)
        settle(mod(block + Z - d, Z), behind[k] if k > 0 else y)
    for d in (1, 7, 2, 6):
        con_wait(d, 0)
    for k in (1, 3, 2):
        for d in (1, 7, 2, 6):
            con_wait(d, k)
    for d in (3, 5, 4):
        for k in (1, 3, 2):
            con_wait(d, k)
    load_interp.wait()
    con_m[...] = con_f[...].astype(BF16)

    def term(to, half):
        tile = interp[pl.ds(to * X, X), half]
        return jnp.dot(
            tile.reshape(-1, tile.shape[-1]), con_m[...], preferred_element_type=F32).reshape(X, *terms.shape[1:])

    order = ((1, 1 - l), (0, l))
    pair = {}
    for i, to in order:
        pair_out[i] = term(to, 1 - core).astype(BF16)
        pair[i] = send(pair_out.at[i], pair_in.at[i], pair_ss.at[i], pair_rs.at[i], sibling)
    fin = {}
    for i, to in order:
        both = term(to, core)
        pair[i].wait_recv()
        both = both + pair_in[i].astype(F32)
        fin_out[i] = both.astype(BF16)
        if i == 0:
            terms[...] = both
        for k in (2, 1, 3, 0):
            if (i, k) != (0, 0):
                fin[i, k] = send(
                    fin_out.at[i, mod(x + k, X)], fin_in.at[i, k], fin_ss.at[i * X + k], fin_rs.at[i * X + k],
                    device(z, y, mod(l + i, L), mod(x + k, X), core))
    total = terms[x]
    for i, k in fin:
        fin[i, k].wait_recv()
        total = total + fin_in[i, k].astype(F32)
    out[...] = total.astype(BF16)

    finish()


def local(orbitals, coulomb, interp):
    h, k = orbitals.shape
    m, n = coulomb.shape
    g = interp.shape[0]
    out = g // (L * X * C)
    dma = pltpu.SemaphoreType.DMA
    return pl.pallas_call(
        kernel,
        out_shape=jax.ShapeDtypeStruct((out, k), BF16),
        in_specs=[
            pl.BlockSpec(memory_space=pltpu.VMEM),
            pl.BlockSpec(memory_space=pltpu.HBM),
            pl.BlockSpec(memory_space=pltpu.HBM),
        ],
        out_specs=pl.BlockSpec(memory_space=pltpu.VMEM),
        scratch_shapes=[
            pltpu.VMEM((m, n), F32),
            pltpu.VMEM((n, m), F32),
            pltpu.VMEM((L * X, C, out, n), BF16),
            pltpu.VMEM((L * X * C, h, k), BF16),
            pltpu.VMEM((m, k), BF16),
            pltpu.VMEM((Z * Y, h, k), BF16),
            pltpu.VMEM((2, 4, Y, h, k), BF16),
            pltpu.VMEM((2, 4, Y, h, k), BF16),
            pltpu.VMEM((Y, h, k), F32),
            pltpu.VMEM((Y, h, k), BF16),
            pltpu.VMEM((Y, h, k), BF16),
            pltpu.VMEM((Z * Y, h, k), BF16),
            pltpu.VMEM((n, k), F32),
            pltpu.VMEM((n, k), BF16),
            pltpu.VMEM((h, k), BF16),
            pltpu.VMEM((X, out, k), F32),
            pltpu.VMEM((L, X, out, k), BF16),
            pltpu.VMEM((L, X, out, k), BF16),
            pltpu.VMEM((L, X, out, k), BF16),
            pltpu.VMEM((L, X, out, k), BF16),
            dma((2,)), dma((2,)), dma((8,)), dma((8,)), dma((8,)), dma((8,)), dma((4,)), dma((4,)),
            dma((2, 4, H)), dma((2, 4, H)), dma((2, 4, H)), dma((2, 4, H)), dma((4,)), dma((4,)),
            dma((Z, Y)), dma((Z, Y)), dma((2,)), dma((2,)), dma((8,)), dma((8,)),
        ],
        compiler_params=pltpu.CompilerParams(
            collective_id=0, has_side_effects=True, vmem_limit_bytes=62 * 1024 * 1024
        ),
        cost_estimate=pl.CostEstimate(
            flops=4 * m * n * k + 2 * g * n * k, bytes_accessed=4 * m * n + 2 * g * n, transcendentals=0
        ),
    )(orbitals, coulomb, interp.reshape(L * X, C, out, n))


def solution(mesh):
    in_specs = (P(("row", "col"), None), P("row", "col"), P("row", "col"))
    out_specs = P(("row", "col"), None)
    return jax.shard_map(local, mesh=mesh, in_specs=in_specs, out_specs=out_specs, check_vma=False)
```
